128 devices in a mesh: dp: 16 (over z_hi, x, core), grad: 8 (over z_lo, y).
Axes of the slice: x: 4, y: 4, z: 4 (z_hi: 2, z_lo: 2; z = z_hi * 2 + z_lo), core: 2. Of those that a mesh axis runs over, the one named last changes fastest.
Arguments:
- inputs: bfloat16 [16384, 4096], P('dp'), may hold values from -6 to 6
- out_grads: bfloat16 [16384, 8192], P('dp'), may hold values from -0.046875 to 0.046875
- basis_g: bfloat16 [4, 2048, 2048], P(None, 'dp'), may hold values from -0.125 to 0.125
- basis_a: bfloat16 [2, 2048, 2048], P(None, 'dp'), may hold values from -0.125 to 0.125
- eig_g: float32 [4, 2048], replicated, may hold values from 0.3 to 3
- eig_a: float32 [2, 2048], replicated, may hold values from 0.3 to 3
Outputs:
- preconditioned: bfloat16 [2048, 8, 2048], P(None, 'grad')
The draws below stay inside these ranges and needn't reach their ends.
All inputs are finite; a program needn't handle non-finite values.
Results may differ from the reference program's by a relative error of at most 0.024.
Values may be sent and summed in bfloat16 or wider, within the bound.
A program may use at most 128 MiB of HBM per device.

```python
import math
import jax
import jax.numpy as jnp
from jax import lax

D = 4096
H = 8192
BS = 2048
TOK_DEV = 1024
NA = 2
NG = 4
TOKENS = 16384
N_DP = 16


def with_spikes(drawn, key, source, target, parts, factor):
    def block_of(position):
        return (jnp.arange(drawn.shape[position]) // (drawn.shape[position] // parts)).reshape((-1,) + (1,) * (drawn.ndim - 1 - position))

    near = jax.random.permutation(key, parts)[block_of(target)]
    other_side = (block_of(target) + parts // 2) % parts
    return jnp.where((block_of(source) == near) | (block_of(source) == other_side), factor * drawn, drawn)


def steps_of(key, extent, cuts, least, top_value):
    def one(axis_at, shards_of):
        draws = jax.random.uniform(jax.random.fold_in(jax.random.fold_in(key, 6), axis_at), (shards_of,), jnp.float32, least / len(cuts), top_value / len(cuts))
        return jnp.repeat(jnp.exp(draws), extent[axis_at] // shards_of).reshape((-1,) + (1,) * (len(extent) - axis_at - 1))

    gain = one(*cuts[0])
    for cut in cuts[1:]:
        gain = gain * one(*cut)
    return gain


def normal_values(own_key, extent, deviation, limit, pieces=(), dtype=jnp.bfloat16):
    factor_of = steps_of(own_key, extent, pieces, -0.22, 0.18) if pieces else 1.0
    values = jax.random.normal(own_key, extent, jnp.float32) * deviation * factor_of
    return jnp.minimum(jnp.maximum(values, -limit), limit).astype(dtype)


def bell_draw_with(rng, extent, scale, bound, pieces, heavy, kind=jnp.bfloat16):
    entries = scale * jax.random.normal(rng, extent, jnp.float32)
    if pieces:
        entries = entries * steps_of(rng, extent, pieces, -0.22, 0.18)
    return jnp.clip(with_spikes(entries, jax.random.fold_in(rng, 3), *heavy), -bound, bound).astype(kind)


def setup_inputs(seed: int = 0) -> dict:
    splits = jax.random.split(jax.random.key(seed), 7)
    inputs = bell_draw_with(splits[0], (TOKENS, D), 1.0, 6.0, ((0, 16),), (0, 1, 16, 2.0))
    out_grads = normal_values(splits[1], (TOKENS, H), (1.0 / (TOK_DEV * N_DP) ** 0.5), 0.046875, ((0, 16),))
    basis_g = normal_values(splits[2], (NG, BS, BS), BS ** -0.5, 0.125, ((1, 16),))
    basis_a = normal_values(splits[3], (NA, BS, BS), BS ** -0.5, 0.125, ((1, 16),))
    eig_g = jnp.clip(jnp.exp(jax.random.uniform(splits[4], (NG, BS), jnp.float32, math.log(0.3), math.log(3.0))), 0.3, 3.0)
    eig_a = jnp.clip(jnp.exp(jax.random.uniform(splits[5], (NA, BS), jnp.float32, math.log(0.3), math.log(3.0))), 0.3, 3.0)
    return dict(inputs=inputs, out_grads=out_grads, basis_g=basis_g, basis_a=basis_a, eig_g=eig_g, eig_a=eig_a)


DAMPING = 0.05


def mat(left, right):
    return jnp.dot(left.astype(jnp.float32), right.astype(jnp.float32), precision=lax.Precision.HIGHEST)


def reference(inputs, out_grads, basis_g, basis_a, eig_g, eig_a):
    groups_x = inputs.reshape(N_DP, TOK_DEV, D)
    groups_y = out_grads.reshape(N_DP, TOK_DEV, H)

    def accumulate(total, pair):
        part = mat(pair[0].T, pair[1]).astype(jnp.bfloat16)
        part = lax.optimization_barrier(part)
        return total + part.astype(jnp.float32), None

    summed, unused = lax.scan(accumulate, jnp.zeros((D, H), jnp.float32), (groups_x, groups_y))
    weight_grad = summed.astype(jnp.bfloat16)
    tiles = []
    for j in range(NA):
        for i in range(NG):
            block = weight_grad[j * BS:(j + 1) * BS, i * BS:(i + 1) * BS]
            rotated = mat(block, basis_g[i]).astype(jnp.bfloat16)
            inner = mat(basis_a[j].T, rotated)
            scaled = (inner / (eig_a[j][:, None] * eig_g[i][None, :] + DAMPING)).astype(jnp.bfloat16)
            back = mat(basis_a[j], scaled).astype(jnp.bfloat16)
            tiles.append(mat(back, basis_g[i].T).astype(jnp.bfloat16))
    return jnp.stack(tiles, axis=1)
```

```python
import functools

import jax
import jax.numpy as jnp
from jax import lax
from jax.experimental import pallas as pl
from jax.experimental.pallas import tpu as pltpu
from jax.sharding import PartitionSpec as P

DAMPING = 0.05
MESH = pl.DeviceIdType.MESH
BF, F32 = jnp.bfloat16, jnp.float32

NX, NZ, NY, NC = 4, 2, 4, 2
CH = NX * NZ
W = 2048
SH = W // (CH * NC)
HALF = W // NC
HS = SH // 2
TOK = 1024
BG_A = 5
RS_A = 768
R = 4
RC = W // R
AG_A = 304
N_SEM = 160


def nn(a, b):
    return lax.dot_general(a, b, (((1,), (0,)), ((), ())), preferred_element_type=F32)


def nt(a, b):
    return lax.dot_general(a, b, (((1,), (1,)), ((), ())), preferred_element_type=F32)


def row_of(table, k):
    rows = lax.broadcasted_iota(jnp.int32, table.shape, 0)
    return jnp.sum(jnp.where(rows == k, table, 0.0), axis=0, keepdims=True)


def kernel(x_hbm, y_hbm, bg_hbm, ba_hbm, eg_ref, ea_ref, out_hbm,
           xb, yb, bgs, tpeer, bgt, ba, ygt, vt, ra, rb, sa, sb, ra2, rb2, vtf, sct, back,
           ss, rs, ls):
    d = lax.axis_index("dp")
    g = lax.axis_index("grad")
    c = lax.rem(d, NC)
    x = lax.rem(lax.div(d, NC), NX)
    zh = lax.div(d, NC * NX)
    y = lax.rem(g, NY)
    zl = lax.div(g, NY)
    q = zh * NX + x

    def dp_of(z_, x_, c_):
        return (z_ * NX + x_) * NC + c_

    xs = [lax.rem(x + k, NX) for k in range(1, NX)]
    xf = [lax.rem(x + NX - k, NX) for k in range(1, NX)]
    to_x = [(dp_of(zh, p, c), g) for p in xs]
    to_z = (dp_of(1 - zh, x, c), g)
    to_c = (dp_of(zh, x, 1 - c), g)
    ys = [lax.rem(y + k, NY) for k in range(1, NY)]
    yf = [lax.rem(y + NY - k, NY) for k in range(1, NY)]
    to_y = [(d, zl * NY + p) for p in ys]

    sends = []
    count = [0]

    def slot():
        count[0] += 1
        return count[0] - 1

    def put(src, dst, dev):
        k = slot()
        cp = pltpu.make_async_remote_copy(src_ref=src, dst_ref=dst, send_sem=ss.at[k], recv_sem=rs.at[k],
                                          device_id=dev, device_id_type=MESH)
        cp.start()
        sends.append(cp)
        return k

    def got(k, dst):
        pltpu.make_async_remote_copy(src_ref=dst, dst_ref=dst, send_sem=ss.at[k], recv_sem=rs.at[k],
                                     device_id=to_c, device_id_type=MESH).wait_recv()

    load_bg = pltpu.make_async_copy(bg_hbm.at[y], bgs, ls.at[0])
    load_bg.start()
    x_src = x_hbm.at[:, pl.ds(pl.multiple_of(zl * W, W), W)]
    y_src = y_hbm.at[:, pl.ds(pl.multiple_of(y * W, W), W)]
    my_tok = pl.ds(pl.multiple_of(c * TOK, TOK), TOK)
    other_tok = pl.ds(pl.multiple_of((1 - c) * TOK, TOK), TOK)
    load_y = pltpu.make_async_copy(y_src, yb.at[my_tok], ls.at[1])
    load_x = pltpu.make_async_copy(x_src, xb.at[my_tok], ls.at[2])
    quarter = pl.ds(pl.multiple_of(y * (SH // NY), SH // NY), SH // NY)
    load_ba = pltpu.make_async_copy(ba_hbm.at[zl, quarter], ba.at[zh, x, c, y], ls.at[3])
    load_ba.start()

    barrier = pltpu.get_barrier_semaphore()
    partners = [*to_x, to_z, to_c, *to_y]
    for dev in partners:
        pl.semaphore_signal(barrier, inc=1, device_id=dev, device_id_type=MESH)
    pl.semaphore_wait(barrier, len(partners))

    load_bg.wait()
    my_lane = pl.ds(pl.multiple_of(q * 2 * SH + c * SH, SH), SH)
    peer_lane = pl.ds(pl.multiple_of(q * 2 * SH + (1 - c) * SH, SH), SH)

    def flip(p, _):
        mine = pl.ds(pl.multiple_of(c * HALF + p * SH, SH), SH)
        other = pl.ds(pl.multiple_of((1 - c) * HALF + p * SH, SH), SH)
        tpeer[p] = bgs[:, other].astype(F32).T.astype(BF)
        bgt[c, p, :, my_lane] = bgs[:, mine].astype(F32).T.astype(BF)
        return 0

    lax.fori_loop(0, CH, flip, 0)
    k_peer = put(tpeer, bgt.at[1 - c, :, :, my_lane], to_c)
    load_y.start()
    load_x.start()
    got(k_peer, bgt.at[c, :, :, peer_lane])

    def bg_piece(side, first, last, h, lanes):
        return bgt.at[side, first:last, pl.ds(h * HS, HS), lanes]

    def lanes_of(z_, x_):
        return pl.ds(pl.multiple_of((z_ * NX + x_) * 2 * SH, 2 * SH), 2 * SH)

    def bg_one(h):
        lane = lanes_of(zh, x)
        kb = put(bg_piece(c, BG_A, CH, h, lane), bg_piece(c, BG_A, CH, h, lane), to_z)
        ka = [put(bg_piece(c, 0, BG_A, h, lane), bg_piece(c, 0, BG_A, h, lane), dev) for dev in to_x]
        return ka, kb

    row_lanes = [pl.ds(pl.multiple_of(z_ * NX * 2 * SH, NX * 2 * SH), NX * 2 * SH) for z_ in (zh, 1 - zh)]

    def bg_two(h, ks):
        ka, kb = ks
        got(kb, bg_piece(c, BG_A, CH, h, lanes_of(1 - zh, x)))
        out = []
        for z_ in (zh, 1 - zh):
            lane = lanes_of(z_, x)
            out.append([put(bg_piece(c, BG_A, CH, h, lane), bg_piece(c, BG_A, CH, h, lane), dev) for dev in to_x])
        for n in range(NX - 1):
            got(ka[n], bg_piece(c, 0, BG_A, h, lanes_of(zh, xf[n])))
        k = put(bg_piece(c, 0, BG_A, h, row_lanes[0]), bg_piece(c, 0, BG_A, h, row_lanes[0]), to_z)
        return out, k

    def bg_done(h, ks):
        kb, ka = ks
        for z_, row in zip((zh, 1 - zh), kb):
            for n in range(NX - 1):
                got(row[n], bg_piece(c, BG_A, CH, h, lanes_of(z_, xf[n])))
        got(ka, bg_piece(c, 0, BG_A, h, row_lanes[1]))

    first0 = bg_one(0)
    k_y = put(y_src, yb.at[my_tok], to_c)
    k_x = put(x_src, xb.at[my_tok], to_c)

    load_ba.wait()

    def ba_piece(z_, x_, first, last):
        return ba.at[z_, x_, c, y, first:last]

    ka_b = put(ba_piece(zh, x, 16, 32), ba_piece(zh, x, 16, 32), to_z)
    ka_a = [put(ba_piece(zh, x, 0, 16), ba_piece(zh, x, 0, 16), dev) for dev in to_x]
    second0 = bg_two(0, first0)
    first1 = bg_one(1)
    got(ka_b, ba_piece(1 - zh, x, 16, 32))
    ka_b2 = [put(ba.at[:, x, c, y, 16:32], ba.at[:, x, c, y, 16:32], dev) for dev in to_x]
    for n in range(NX - 1):
        got(ka_a[n], ba_piece(zh, xf[n], 0, 16))
    ka_a2 = put(ba.at[zh, :, c, y, 0:16], ba.at[zh, :, c, y, 0:16], to_z)
    second1 = bg_two(1, first1)
    for n in range(NX - 1):
        got(ka_b2[n], ba.at[:, xf[n], c, y, 16:32])
    got(ka_a2, ba.at[1 - zh, :, c, y, 0:16])
    ka_y = [put(ba.at[:, :, c, y], ba.at[:, :, c, y], dev) for dev in to_y]

    load_y.wait()
    load_x.wait()
    got(k_y, yb.at[other_tok])
    got(k_x, xb.at[other_tok])

    def grad(h):
        def rotate(t, _):
            rows = pl.ds(pl.multiple_of(t * 256, 256), 256)
            left = bgt[c, :, pl.ds(h * HS, HS), :].reshape(CH * HS, W)
            ygt[:, rows] = nt(left, yb[rows, :]).astype(BF)
            return 0

        lax.fori_loop(0, NC * TOK // 256, rotate, 0)

        def project(t, _):
            cols = pl.ds(pl.multiple_of(t * 256, 256), 256)
            vt[h, :, :, :, cols] = nn(ygt[...], xb[:, cols]).astype(BF).reshape(NZ, NX, HS, 256)
            return 0

        lax.fori_loop(0, W // 256, project, 0)

    A, B = pl.ds(0, RS_A), pl.ds(RS_A, W - RS_A)

    def rs_one(h):
        kb = put(vt.at[h, 1 - zh, :, :, B], rb.at[h], to_z)
        ka = [put(vt.at[h, :, p, :, A], ra.at[h, n], dev) for n, (p, dev) in enumerate(zip(xs, to_x))]
        return ka, kb

    def rs_two(h, ks):
        ka, kb = ks
        got(kb, rb.at[h])
        sb[h] = (vt[h, zh, :, :, B].astype(F32) + rb[h].astype(F32)).astype(BF)
        kb2 = [put(sb.at[h, p], rb2.at[h, n], dev) for n, (p, dev) in enumerate(zip(xs, to_x))]
        for n in range(NX - 1):
            got(ka[n], ra.at[h, n])

        def total(z_):
            t = vt[h, z_, x, :, A].astype(F32)
            for n in range(NX - 1):
                t = t + ra[h, n, z_].astype(F32)
            return t

        sa[h] = total(1 - zh).astype(BF)
        ka2 = put(sa.at[h], ra2.at[h], to_z)
        vtf[pl.ds(h * HS, HS), A] = total(zh)
        return ka2, kb2

    def rs_done(h, ks):
        ka2, kb2 = ks
        rows = pl.ds(h * HS, HS)
        t = sb[h, x].astype(F32)
        for n in range(NX - 1):
            got(kb2[n], rb2.at[h, n])
            t = t + rb2[h, n].astype(F32)
        vtf[rows, B] = t
        got(ka2, ra2.at[h])
        vtf[rows, A] = vtf[rows, A] + ra2[h].astype(F32)

    bg_done(0, second0)
    grad(0)
    r0 = rs_one(0)
    bg_done(1, second1)
    k_bg = put(bgt.at[c], bgt.at[c], to_c)
    grad(1)
    r1 = rs_one(1)
    for n in range(NY - 1):
        got(ka_y[n], ba.at[:, :, c, yf[n]])
    k_ba = put(ba.at[:, :, c], ba.at[:, :, c], to_c)
    r0 = rs_two(0, r0)
    r1 = rs_two(1, r1)
    got(k_ba, ba.at[:, :, 1 - c])
    rs_done(0, r0)
    rs_done(1, r1)

    own = vtf[...].astype(BF)
    my_m = pl.ds(pl.multiple_of(c * HALF + q * SH, SH), SH)
    lam_g = jnp.broadcast_to(row_of(eg_ref[:, my_m], y), (SH, SH)).T[:, 0:1]
    vtb = sct
    vtb[0] = own

    def scale(t, _):
        cols = pl.ds(pl.multiple_of(t * 256, 256), 256)
        inner = nn(vtb[0], ba[:, :, :, :, :, cols].reshape(W, 256))
        lam = row_of(ea_ref[:, cols], zl)
        vtb[1, :, cols] = (inner / (lam_g * lam + DAMPING)).astype(BF)
        return 0

    lax.fori_loop(0, W // 256, scale, 0)

    def back_rows(r):
        left = ba[r * NZ // R, pl.ds((r * CH // R) % NX, CH // R)].reshape(RC, W)
        back[c, zh, x, pl.ds(r * RC, RC), :] = nt(left, vtb[1]).astype(BF)

    def ag_rows(r):
        return pl.ds(r * RC, AG_A), pl.ds(r * RC + AG_A, RC - AG_A)

    def ag_one(r):
        ra_, rb_ = ag_rows(r)
        kb = put(back.at[c, zh, x, rb_], back.at[c, zh, x, rb_], to_z)
        ka = [put(back.at[c, zh, x, ra_], back.at[c, zh, x, ra_], dev) for dev in to_x]
        return ka, kb

    def ag_two(r, ks):
        ka, kb = ks
        ra_, rb_ = ag_rows(r)
        got(kb, back.at[c, 1 - zh, x, rb_])
        kb2 = [put(back.at[c, :, x, rb_], back.at[c, :, x, rb_], dev) for dev in to_x]
        for n in range(NX - 1):
            got(ka[n], back.at[c, zh, xf[n], ra_])
        ka2 = put(back.at[c, zh, :, ra_], back.at[c, zh, :, ra_], to_z)
        return ka2, kb2

    def ag_core(r, ks):
        ka2, kb2 = ks
        ra_, rb_ = ag_rows(r)
        got(ka2, back.at[c, 1 - zh, :, ra_])
        for n in range(NX - 1):
            got(kb2[n], back.at[c, :, xf[n], rb_])
        rows = pl.ds(r * RC, RC)
        return put(back.at[c, :, :, rows], back.at[c, :, :, rows], to_c)

    outs = []

    def finish(r, k):
        rows = pl.ds(r * RC, RC)
        got(k, back.at[1 - c, :, :, rows])

        def block(t, _):
            cols = pl.ds(pl.multiple_of(t * 256, 256), 256)
            left = jnp.concatenate([back[k // CH, (k // NX) % NZ, k % NX, rows, :] for k in range(NC * CH)], axis=1)
            right = bgt[:, :, :, cols].reshape(W, 256)
            xb[rows, cols] = nn(left, right).astype(BF)
            return 0

        lax.fori_loop(0, W // 256, block, 0)
        cp = pltpu.make_async_copy(xb.at[rows], out_hbm.at[rows], ls.at[8 + r])
        cp.start()
        outs.append(cp)

    k1, k2, k3 = {}, {}, {}
    for r in range(R):
        back_rows(r)
        if r < 2:
            k1[r] = ag_one(r)
    got(k_bg, bgt.at[1 - c])
    for r in range(R):
        k2[r] = ag_two(r, k1[r])
        if r + 2 < R:
            k1[r + 2] = ag_one(r + 2)
        if r >= 1:
            k3[r - 1] = ag_core(r - 1, k2[r - 1])
        if r >= 2:
            finish(r - 2, k3[r - 2])
    k3[R - 1] = ag_core(R - 1, k2[R - 1])
    for r in range(R - 2, R):
        finish(r, k3[r])
    for cp in outs:
        cp.wait()
    for cp in sends:
        cp.wait_send()


def body(inputs, out_grads, basis_g, basis_a, eig_g, eig_a):
    out = pl.pallas_call(
        kernel,
        out_shape=jax.ShapeDtypeStruct((W, W), BF),
        in_specs=[pl.BlockSpec(memory_space=pl.ANY)] * 4 + [pl.BlockSpec(memory_space=pltpu.VMEM)] * 2,
        out_specs=pl.BlockSpec(memory_space=pl.ANY),
        scratch_shapes=[
            pltpu.VMEM((NC * TOK, W), BF),
            pltpu.VMEM((NC * TOK, W), BF),
            pltpu.VMEM((SH, W), BF),
            pltpu.VMEM((CH, SH, SH), BF),
            pltpu.VMEM((NC, CH, SH, W), BF),
            pltpu.VMEM((NZ, NX, NC, NY, SH // NY, W), BF),
            pltpu.VMEM((CH * HS, NC * TOK), BF),
            pltpu.VMEM((2, NZ, NX, HS, W), BF),
            pltpu.VMEM((2, NX - 1, NZ, HS, RS_A), BF),
            pltpu.VMEM((2, NX, HS, W - RS_A), BF),
            pltpu.VMEM((2, HS, RS_A), BF),
            pltpu.VMEM((2, NX, HS, W - RS_A), BF),
            pltpu.VMEM((2, HS, RS_A), BF),
            pltpu.VMEM((2, NX - 1, HS, W - RS_A), BF),
            pltpu.VMEM((SH, W), F32),
            pltpu.VMEM((2, SH, W), BF),
            pltpu.VMEM((NC, NZ, NX, W, SH), BF),
            pltpu.SemaphoreType.DMA((N_SEM,)),
            pltpu.SemaphoreType.DMA((N_SEM,)),
            pltpu.SemaphoreType.DMA((8 + R,)),
        ],
        compiler_params=pltpu.CompilerParams(collective_id=0, has_side_effects=True, vmem_limit_bytes=60 * 2**20),
        cost_estimate=pl.CostEstimate(flops=2 * W * W * W * 3, bytes_accessed=40 * 2**20, transcendentals=0),
        name="precondition",
    )(inputs, out_grads, basis_g, basis_a, eig_g, eig_a)
    return out.reshape(W, 1, W)


def solution(mesh):
    in_specs = (P("dp", None), P("dp", None), P(None, "dp", None), P(None, "dp", None), P(), P())
    out_specs = P(None, "grad", None)
    return jax.shard_map(body, mesh=mesh, in_specs=in_specs, out_specs=out_specs, check_vma=False)
```

```python
import functools

import jax
import jax.numpy as jnp
from jax import lax
from jax.experimental import pallas as pl
from jax.experimental.pallas import tpu as pltpu
from jax.sharding import PartitionSpec as P

DAMPING = 0.05
MESH = pl.DeviceIdType.MESH
BF, F32 = jnp.bfloat16, jnp.float32

NX, NZ, NY, NC = 4, 2, 4, 2
CH = NX * NZ
W = 2048
SH = W // (CH * NC)
HALF = W // NC
HS = SH // 2
TOK = 1024
BG_A = 4
RS_A = 768
R = 4
RC = W // R
AG_A = 224
N_SEM = 160


def nn(a, b):
    return lax.dot_general(a, b, (((1,), (0,)), ((), ())), preferred_element_type=F32)


def nt(a, b):
    return lax.dot_general(a, b, (((1,), (1,)), ((), ())), preferred_element_type=F32)


def row_of(table, k):
    rows = lax.broadcasted_iota(jnp.int32, table.shape, 0)
    return jnp.sum(jnp.where(rows == k, table, 0.0), axis=0, keepdims=True)


def kernel(x_hbm, y_hbm, bg_hbm, ba_hbm, eg_ref, ea_ref, out_hbm,
           xb, yb, bgs, tpeer, bgt, ba, ygt, vt, rz, rbd, rod, rbf, rof, rzb, vtf, sct, back,
           ss, rs, ls):
    d = lax.axis_index("dp")
    g = lax.axis_index("grad")
    c = lax.rem(d, NC)
    x = lax.rem(lax.div(d, NC), NX)
    zh = lax.div(d, NC * NX)
    y = lax.rem(g, NY)
    zl = lax.div(g, NY)
    q = zh * NX + x

    def dp_of(z_, x_, c_):
        return (z_ * NX + x_) * NC + c_

    xp, xm, x2 = lax.rem(x + 1, NX), lax.rem(x + NX - 1, NX), lax.rem(x + 2, NX)
    to_xp, to_xm = (dp_of(zh, xp, c), g), (dp_of(zh, xm, c), g)
    to_z = (dp_of(1 - zh, x, c), g)
    to_c = (dp_of(zh, x, 1 - c), g)
    yp, ym, y2 = lax.rem(y + 1, NY), lax.rem(y + NY - 1, NY), lax.rem(y + 2, NY)
    to_yp, to_ym = (d, zl * NY + yp), (d, zl * NY + ym)

    sends = []
    count = [0]

    def slot():
        count[0] += 1
        return count[0] - 1

    def put(src, dst, dev):
        k = slot()
        cp = pltpu.make_async_remote_copy(src_ref=src, dst_ref=dst, send_sem=ss.at[k], recv_sem=rs.at[k],
                                          device_id=dev, device_id_type=MESH)
        cp.start()
        sends.append(cp)
        return k

    def got(k, dst):
        pltpu.make_async_remote_copy(src_ref=dst, dst_ref=dst, send_sem=ss.at[k], recv_sem=rs.at[k],
                                     device_id=to_c, device_id_type=MESH).wait_recv()

    load_bg = pltpu.make_async_copy(bg_hbm.at[y], bgs, ls.at[0])
    load_bg.start()
    x_src = x_hbm.at[:, pl.ds(pl.multiple_of(zl * W, W), W)]
    y_src = y_hbm.at[:, pl.ds(pl.multiple_of(y * W, W), W)]
    my_tok = pl.ds(pl.multiple_of(c * TOK, TOK), TOK)
    other_tok = pl.ds(pl.multiple_of((1 - c) * TOK, TOK), TOK)
    load_y = pltpu.make_async_copy(y_src, yb.at[my_tok], ls.at[1])
    load_x = pltpu.make_async_copy(x_src, xb.at[my_tok], ls.at[2])
    quarter = pl.ds(pl.multiple_of(y * (SH // NY), SH // NY), SH // NY)
    load_ba = pltpu.make_async_copy(ba_hbm.at[zl, quarter], ba.at[zh, x, c, y], ls.at[3])
    load_ba.start()

    barrier = pltpu.get_barrier_semaphore()
    partners = [to_xp, to_xm, to_z, to_c, to_yp, to_ym]
    for dev in partners:
        pl.semaphore_signal(barrier, inc=1, device_id=dev, device_id_type=MESH)
    pl.semaphore_wait(barrier, len(partners))

    class Gather:
        def __init__(self, ref, n, a, m, mb):
            self.ref, self.n, self.a, self.m, self.mb = ref, n, a, m, mb

        def move(self, z_, x_, first, last, dev):
            return put(self.ref(z_, x_, first, last), self.ref(z_, x_, first, last), dev)

        def one(self):
            self.p = self.move(zh, x, 0, self.n, to_xp)
            self.q = self.move(zh, x, 0, self.n, to_xm)
            self.z = self.move(zh, x, 0, self.n, to_z)

        def two(self):
            n, a, m = self.n, self.a, self.m
            got(self.p, self.ref(zh, xm, 0, n))
            self.p2 = self.move(zh, xm, 0, m, to_xp)
            self.zp = self.move(zh, xm, 0, a, to_z)
            got(self.q, self.ref(zh, xp, 0, n))
            self.q2 = self.move(zh, xp, m, n, to_xm)
            self.zq = self.move(zh, xp, 0, a, to_z)
            got(self.z, self.ref(1 - zh, x, 0, n))
            self.pb = self.move(1 - zh, x, a, n, to_xp)
            self.qb = self.move(1 - zh, x, a, n, to_xm)

        def three(self):
            n, a, m, mb = self.n, self.a, self.m, self.mb
            got(self.p2, self.ref(zh, x2, 0, m))
            self.z2 = self.move(zh, x2, 0, a, to_z)
            got(self.pb, self.ref(1 - zh, xm, a, n))
            self.pb2 = self.move(1 - zh, xm, a, mb, to_xp)
            got(self.qb, self.ref(1 - zh, xp, a, n))
            self.qb2 = self.move(1 - zh, xp, mb, n, to_xm)

        def done(self):
            n, a, m, mb = self.n, self.a, self.m, self.mb
            got(self.q2, self.ref(zh, x2, m, n))
            got(self.zp, self.ref(1 - zh, xm, 0, a))
            got(self.zq, self.ref(1 - zh, xp, 0, a))
            got(self.z2, self.ref(1 - zh, x2, 0, a))
            got(self.pb2, self.ref(1 - zh, x2, a, mb))
            got(self.qb2, self.ref(1 - zh, x2, mb, n))

    load_ba.wait()
    ga = Gather(lambda z_, x_, first, last: ba.at[z_, x_, c, y, :, first:last], W, W // 2, W // 2, 3 * W // 4)
    ga.one()

    load_bg.wait()
    my_lane = pl.ds(pl.multiple_of(q * 2 * SH + c * SH, SH), SH)
    peer_lane = pl.ds(pl.multiple_of(q * 2 * SH + (1 - c) * SH, SH), SH)

    def flip(p, _):
        mine = pl.ds(pl.multiple_of(c * HALF + p * SH, SH), SH)
        other = pl.ds(pl.multiple_of((1 - c) * HALF + p * SH, SH), SH)
        tpeer[p] = bgs[:, other].astype(F32).T.astype(BF)
        bgt[c, p, :, my_lane] = bgs[:, mine].astype(F32).T.astype(BF)
        return 0

    lax.fori_loop(0, CH, flip, 0)
    k_peer = put(tpeer, bgt.at[1 - c, :, :, my_lane], to_c)
    load_y.start()
    load_x.start()
    got(k_peer, bgt.at[c, :, :, peer_lane])

    def bg_ref(h):
        def ref(z_, x_, first, last):
            lanes = pl.ds(pl.multiple_of((z_ * NX + x_) * 2 * SH, 2 * SH), 2 * SH)
            return bgt.at[c, first:last, pl.ds(h * HS, HS), lanes]

        return ref

    gb = [Gather(bg_ref(h), CH, BG_A, CH // 2, (CH + BG_A) // 2) for h in range(2)]
    gb[0].one()
    k_y = put(y_src, yb.at[my_tok], to_c)
    k_x = put(x_src, xb.at[my_tok], to_c)

    def grad(h, first, last):
        def rotate(t, _):
            rows = pl.ds(pl.multiple_of(t * 256, 256), 256)
            left = bgt[c, :, pl.ds(h * HS, HS), :].reshape(CH * HS, W)
            ygt[:, rows] = nt(left, yb[rows, :]).astype(BF)
            return 0

        lax.fori_loop(first, last, rotate, 0)

    def outer(h, first, last):
        def project(t, _):
            cols = pl.ds(pl.multiple_of(t * 256, 256), 256)
            vt[h, :, :, :, cols] = nn(ygt[...], xb[:, cols]).astype(BF).reshape(NZ, NX, HS, 256)
            return 0

        lax.fori_loop(first, last, project, 0)

    A, B = pl.ds(0, RS_A), pl.ds(RS_A, W - RS_A)
    B0, B1 = pl.ds(RS_A, (W - RS_A) // 2), pl.ds((W + RS_A) // 2, (W - RS_A) // 2)
    H0, H1 = pl.ds(0, W // 2), pl.ds(W // 2, W // 2)

    def plus(a, b):
        return (a.astype(F32) + b.astype(F32)).astype(BF)

    class Scatter:
        def __init__(self, h):
            self.h = h

        def one(self):
            h, o = self.h, 1 - zh
            self.z2 = put(vt.at[h, o, x2, :, A], rz.at[h, 0], to_z)
            self.bd0 = put(vt.at[h, o, x2, :, B0], rbd.at[h, 0], to_xp)
            self.bd1 = put(vt.at[h, o, x2, :, B1], rbd.at[h, 1], to_xm)
            self.od1 = put(vt.at[h, zh, x2, :, H1], rod.at[h, 1], to_xm)
            self.zp = put(vt.at[h, o, xp, :, A], rz.at[h, 1], to_z)
            self.zq = put(vt.at[h, o, xm, :, A], rz.at[h, 2], to_z)
            self.zo = put(vt.at[h, o, x, :, A], rz.at[h, 3], to_z)

        def two(self):
            h, o = self.h, 1 - zh
            got(self.z2, rz.at[h, 0])
            vt[h, zh, x2, :, A] = plus(vt[h, zh, x2, :, A], rz[h, 0])
            self.od0 = put(vt.at[h, zh, x2, :, H0], rod.at[h, 0], to_xp)
            got(self.bd0, rbd.at[h, 0])
            vt[h, o, xp, :, B0] = plus(vt[h, o, xp, :, B0], rbd[h, 0])
            self.bf0 = put(vt.at[h, o, xp, :, B], rbf.at[h, 0], to_xp)
            got(self.bd1, rbd.at[h, 1])
            vt[h, o, xm, :, B1] = plus(vt[h, o, xm, :, B1], rbd[h, 1])
            self.bf1 = put(vt.at[h, o, xm, :, B], rbf.at[h, 1], to_xm)

        def three(self):
            h, o = self.h, 1 - zh
            got(self.zq, rz.at[h, 2])
            vt[h, zh, xm, :, A] = plus(vt[h, zh, xm, :, A], rz[h, 2])
            got(self.od1, rod.at[h, 1])
            vt[h, zh, xm, :, H1] = plus(vt[h, zh, xm, :, H1], rod[h, 1])
            self.of1 = put(vt.at[h, zh, xm], rof.at[h, 1], to_xm)
            got(self.zp, rz.at[h, 1])
            vt[h, zh, xp, :, A] = plus(vt[h, zh, xp, :, A], rz[h, 1])
            got(self.od0, rod.at[h, 0])
            vt[h, zh, xp, :, H0] = plus(vt[h, zh, xp, :, H0], rod[h, 0])
            self.of0 = put(vt.at[h, zh, xp], rof.at[h, 0], to_xp)
            got(self.bf0, rbf.at[h, 0])
            got(self.bf1, rbf.at[h, 1])
            t = vt[h, o, x, :, B].astype(F32) + rbf[h, 0].astype(F32) + rbf[h, 1].astype(F32)
            vt[h, o, x, :, B] = t.astype(BF)
            self.zb = put(vt.at[h, o, x, :, B], rzb.at[h], to_z)

        def done(self):
            h = self.h
            got(self.zo, rz.at[h, 3])
            got(self.of0, rof.at[h, 0])
            got(self.of1, rof.at[h, 1])
            got(self.zb, rzb.at[h])
            t = vt[h, zh, x].astype(F32) + rof[h, 0].astype(F32) + rof[h, 1].astype(F32)
            rows = pl.ds(h * HS, HS)
            vtf[rows, A] = t[:, :RS_A] + rz[h, 3].astype(F32)
            vtf[rows, B] = t[:, RS_A:] + rzb[h].astype(F32)

    sc = [Scatter(h) for h in range(2)]

    def ba_part(y_):
        return ba.at[:, :, c, y_]

    def ba_theirs(y_):
        return ba.at[:, :, 1 - c, y_]

    ga.two()
    gb[0].two()
    ga.three()
    gb[1].one()
    ga.done()
    k_yp = put(ba_part(y), ba_part(y), to_yp)
    k_ym = put(ba_part(y), ba_part(y), to_ym)
    gb[0].three()
    gb[1].two()
    load_y.wait()
    load_x.wait()
    got(k_y, yb.at[other_tok])
    got(k_x, xb.at[other_tok])
    k_c = [put(ba_part(y), ba_part(y), to_c)]
    gb[0].done()
    grad(0, 0, 4)
    gb[1].three()
    grad(0, 4, 8)
    outer(0, 0, 8)
    sc[0].one()
    gb[1].done()
    k_bg = put(bgt.at[c], bgt.at[c], to_c)
    got(k_yp, ba_part(ym))
    k_yp2 = put(ba.at[0, :, c, ym], ba.at[0, :, c, ym], to_yp)
    got(k_ym, ba_part(yp))
    k_ym2 = put(ba.at[1, :, c, yp], ba.at[1, :, c, yp], to_ym)
    k_c += [put(ba_part(ym), ba_part(ym), to_c), put(ba_part(yp), ba_part(yp), to_c)]
    grad(1, 0, 8)
    sc[0].two()
    outer(1, 0, 4)
    sc[0].three()
    outer(1, 4, 8)
    sc[1].one()
    got(k_yp2, ba.at[0, :, c, y2])
    got(k_ym2, ba.at[1, :, c, y2])
    k_c.append(put(ba_part(y2), ba_part(y2), to_c))
    sc[1].two()
    sc[0].done()
    sc[1].three()
    for k, y_ in zip(k_c, (y, ym, yp, y2)):
        got(k, ba_theirs(y_))
    sc[1].done()

    own = vtf[...].astype(BF)
    my_m = pl.ds(pl.multiple_of(c * HALF + q * SH, SH), SH)
    lam_g = jnp.broadcast_to(row_of(eg_ref[:, my_m], y), (SH, SH)).T[:, 0:1]
    vtb = sct
    vtb[0] = own

    def scale(t, _):
        cols = pl.ds(pl.multiple_of(t * 256, 256), 256)
        inner = nn(vtb[0], ba[:, :, :, :, :, cols].reshape(W, 256))
        lam = row_of(ea_ref[:, cols], zl)
        vtb[1, :, cols] = (inner / (lam_g * lam + DAMPING)).astype(BF)
        return 0

    lax.fori_loop(0, W // 256, scale, 0)

    def back_rows(r):
        left = ba[r * NZ // R, pl.ds((r * CH // R) % NX, CH // R)].reshape(RC, W)
        back[c, zh, x, pl.ds(r * RC, RC), :] = nt(left, vtb[1]).astype(BF)

    def back_ref(r):
        return lambda z_, x_, first, last: back.at[c, z_, x_, pl.ds(r * RC + first, last - first)]

    gr = [Gather(back_ref(r), RC, AG_A, RC // 2, (RC + AG_A) // 2) for r in range(R)]

    def to_core(r):
        rows = pl.ds(r * RC, RC)
        return put(back.at[c, :, :, rows], back.at[c, :, :, rows], to_c)

    outs = []

    def finish(r, k):
        rows = pl.ds(r * RC, RC)
        got(k, back.at[1 - c, :, :, rows])

        def block(t, _):
            cols = pl.ds(pl.multiple_of(t * 256, 256), 256)
            left = jnp.concatenate([back[k // CH, (k // NX) % NZ, k % NX, rows, :] for k in range(NC * CH)], axis=1)
            right = bgt[:, :, :, cols].reshape(W, 256)
            xb[rows, cols] = nn(left, right).astype(BF)
            return 0

        lax.fori_loop(0, W // 256, block, 0)
        cp = pltpu.make_async_copy(xb.at[rows], out_hbm.at[rows], ls.at[8 + r])
        cp.start()
        outs.append(cp)

    k3 = {}
    for r in range(R):
        back_rows(r)
        if r < 2:
            gr[r].one()
    got(k_bg, bgt.at[1 - c])
    for r in range(R + 3):
        if r < R:
            gr[r].two()
        if 1 <= r <= R:
            gr[r - 1].three()
        if r + 2 < R:
            gr[r + 2].one()
        if 2 <= r <= R + 1:
            gr[r - 2].done()
            k3[r - 2] = to_core(r - 2)
        if r >= 3:
            finish(r - 3, k3[r - 3])
    for cp in outs:
        cp.wait()
    for cp in sends:
        cp.wait_send()


def body(inputs, out_grads, basis_g, basis_a, eig_g, eig_a):
    out = pl.pallas_call(
        kernel,
        out_shape=jax.ShapeDtypeStruct((W, W), BF),
        in_specs=[pl.BlockSpec(memory_space=pl.ANY)] * 4 + [pl.BlockSpec(memory_space=pltpu.VMEM)] * 2,
        out_specs=pl.BlockSpec(memory_space=pl.ANY),
        scratch_shapes=[
            pltpu.VMEM((NC * TOK, W), BF),
            pltpu.VMEM((NC * TOK, W), BF),
            pltpu.VMEM((SH, W), BF),
            pltpu.VMEM((CH, SH, SH), BF),
            pltpu.VMEM((NC, CH, SH, W), BF),
            pltpu.VMEM((NZ, NX, NC, NY, SH // NY, W), BF),
            pltpu.VMEM((CH * HS, NC * TOK), BF),
            pltpu.VMEM((2, NZ, NX, HS, W), BF),
            pltpu.VMEM((2, NX, HS, RS_A), BF),
            pltpu.VMEM((2, 2, HS, (W - RS_A) // 2), BF),
            pltpu.VMEM((2, 2, HS, W // 2), BF),
            pltpu.VMEM((2, 2, HS, W - RS_A), BF),
            pltpu.VMEM((2, 2, HS, W), BF),
            pltpu.VMEM((2, HS, W - RS_A), BF),
            pltpu.VMEM((SH, W), F32),
            pltpu.VMEM((2, SH, W), BF),
            pltpu.VMEM((NC, NZ, NX, W, SH), BF),
            pltpu.SemaphoreType.DMA((N_SEM,)),
            pltpu.SemaphoreType.DMA((N_SEM,)),
            pltpu.SemaphoreType.DMA((8 + R,)),
        ],
        compiler_params=pltpu.CompilerParams(collective_id=0, has_side_effects=True, vmem_limit_bytes=60 * 2**20),
        cost_estimate=pl.CostEstimate(flops=2 * W * W * W * 3, bytes_accessed=40 * 2**20, transcendentals=0),
        name="precondition",
    )(inputs, out_grads, basis_g, basis_a, eig_g, eig_a)
    return out.reshape(W, 1, W)


def solution(mesh):
    in_specs = (P("dp", None), P("dp", None), P(None, "dp", None), P(None, "dp", None), P(), P())
    out_specs = P(None, "grad", None)
    return jax.shard_map(body, mesh=mesh, in_specs=in_specs, out_specs=out_specs, check_vma=False)
```

```python
import functools

import jax
import jax.numpy as jnp
from jax import lax
from jax.experimental import pallas as pl
from jax.experimental.pallas import tpu as pltpu
from jax.sharding import PartitionSpec as P

DAMPING = 0.05
MESH = pl.DeviceIdType.MESH
BF, F32 = jnp.bfloat16, jnp.float32

NX, NZ, NY, NC = 4, 2, 4, 2
CH = NX * NZ
W = 2048
SH = W // (CH * NC)
HALF = W // NC
HS = SH // 2
TOK = 1024
BG_A = 4
RS_A = 768
WIDE = 512
SIZE = (512, 512, 512, 256, 256)
R = len(SIZE)
ROWS = tuple(sum(SIZE[:r]) for r in range(R))
LAST_Z = tuple(n * 7 // 16 // 32 * 32 for n in SIZE)
N_SEM = 160
PARTS = 8


def nn(a, b):
    return lax.dot_general(a, b, (((1,), (0,)), ((), ())), preferred_element_type=F32)


def nt(a, b):
    return lax.dot_general(a, b, (((1,), (1,)), ((), ())), preferred_element_type=F32)


def row_of(table, k):
    rows = lax.broadcasted_iota(jnp.int32, table.shape, 0)
    return jnp.sum(jnp.where(rows == k, table, 0.0), axis=0, keepdims=True)


def kernel(x_hbm, y_hbm, bg_hbm, ba_hbm, eg_ref, ea_ref, xb,
           yb, bgs, tpeer, bgt, ba, ygt, vt, rz, rbd, rod, rbf, rof, rzb, vtf, sct, back,
           ss, rs, ls):
    d = lax.axis_index("dp")
    g = lax.axis_index("grad")
    c = lax.rem(d, NC)
    x = lax.rem(lax.div(d, NC), NX)
    zh = lax.div(d, NC * NX)
    y = lax.rem(g, NY)
    zl = lax.div(g, NY)
    q = zh * NX + x

    def dp_of(z_, x_, c_):
        return (z_ * NX + x_) * NC + c_

    xp, xm, x2 = lax.rem(x + 1, NX), lax.rem(x + NX - 1, NX), lax.rem(x + 2, NX)
    to_xp, to_xm = (dp_of(zh, xp, c), g), (dp_of(zh, xm, c), g)
    to_z = (dp_of(1 - zh, x, c), g)
    to_c = (dp_of(zh, x, 1 - c), g)
    yp, ym, y2 = lax.rem(y + 1, NY), lax.rem(y + NY - 1, NY), lax.rem(y + 2, NY)
    to_yp, to_ym = (d, zl * NY + yp), (d, zl * NY + ym)

    sends = []
    count = [0]

    def slot():
        count[0] += 1
        return count[0] - 1

    def put(src, dst, dev):
        k = slot()
        cp = pltpu.make_async_remote_copy(src_ref=src, dst_ref=dst, send_sem=ss.at[k], recv_sem=rs.at[k],
                                          device_id=dev, device_id_type=MESH)
        cp.start()
        sends.append(cp)
        return k

    def got(k, dst):
        pltpu.make_async_remote_copy(src_ref=dst, dst_ref=dst, send_sem=ss.at[k], recv_sem=rs.at[k],
                                     device_id=to_c, device_id_type=MESH).wait_recv()

    load_bg = pltpu.make_async_copy(bg_hbm.at[y], bgs, ls.at[0])
    load_bg.start()
    x_src = x_hbm.at[:, pl.ds(pl.multiple_of(zl * W, W), W)]
    y_src = y_hbm.at[:, pl.ds(pl.multiple_of(y * W, W), W)]
    my_tok = pl.ds(pl.multiple_of(c * TOK, TOK), TOK)
    other_tok = pl.ds(pl.multiple_of((1 - c) * TOK, TOK), TOK)
    load_y = pltpu.make_async_copy(y_src, yb.at[my_tok], ls.at[1])
    load_x = pltpu.make_async_copy(x_src, xb.at[my_tok], ls.at[2])
    quarter = pl.ds(pl.multiple_of(y * (SH // NY), SH // NY), SH // NY)
    load_ba = pltpu.make_async_copy(ba_hbm.at[zl, quarter], ba.at[zh, x, c, y], ls.at[3])
    load_ba.start()

    barrier = pltpu.get_barrier_semaphore()
    partners = [to_xp, to_xm, to_z, to_c, to_yp, to_ym]
    for dev in partners:
        pl.semaphore_signal(barrier, inc=1, device_id=dev, device_id_type=MESH)
    pl.semaphore_wait(barrier, len(partners))

    class Gather:
        def __init__(self, ref, n, a, m, mb):
            self.ref, self.n, self.a, self.m, self.mb = ref, n, a, m, mb

        def move(self, z_, x_, first, last, dev):
            return put(self.ref(z_, x_, first, last), self.ref(z_, x_, first, last), dev)

        def one(self):
            self.p = self.move(zh, x, 0, self.n, to_xp)
            self.q = self.move(zh, x, 0, self.n, to_xm)
            self.z = self.move(zh, x, 0, self.n, to_z)

        def two(self):
            n, a, m = self.n, self.a, self.m
            got(self.p, self.ref(zh, xm, 0, n))
            self.p2 = self.move(zh, xm, 0, m, to_xp)
            self.zp = self.move(zh, xm, 0, a, to_z)
            got(self.q, self.ref(zh, xp, 0, n))
            self.q2 = self.move(zh, xp, m, n, to_xm)
            self.zq = self.move(zh, xp, 0, a, to_z)
            got(self.z, self.ref(1 - zh, x, 0, n))
            self.pb = self.move(1 - zh, x, a, n, to_xp)
            self.qb = self.move(1 - zh, x, a, n, to_xm)

        def three(self):
            n, a, m, mb = self.n, self.a, self.m, self.mb
            got(self.p2, self.ref(zh, x2, 0, m))
            self.z2 = self.move(zh, x2, 0, a, to_z)
            got(self.pb, self.ref(1 - zh, xm, a, n))
            self.pb2 = self.move(1 - zh, xm, a, mb, to_xp)
            got(self.qb, self.ref(1 - zh, xp, a, n))
            self.qb2 = self.move(1 - zh, xp, mb, n, to_xm)

        def done(self):
            n, a, m, mb = self.n, self.a, self.m, self.mb
            got(self.q2, self.ref(zh, x2, m, n))
            got(self.zp, self.ref(1 - zh, xm, 0, a))
            got(self.zq, self.ref(1 - zh, xp, 0, a))
            got(self.z2, self.ref(1 - zh, x2, 0, a))
            got(self.pb2, self.ref(1 - zh, x2, a, mb))
            got(self.qb2, self.ref(1 - zh, x2, mb, n))

    load_ba.wait()
    ga = Gather(lambda z_, x_, first, last: ba.at[z_, x_, c, y, :, first:last], W, W // 2, W // 2, 3 * W // 4)
    ga.one()

    load_bg.wait()
    my_lane = pl.ds(pl.multiple_of(q * 2 * SH + c * SH, SH), SH)
    peer_lane = pl.ds(pl.multiple_of(q * 2 * SH + (1 - c) * SH, SH), SH)

    def flip(p, _):
        mine = pl.ds(pl.multiple_of(c * HALF + p * SH, SH), SH)
        other = pl.ds(pl.multiple_of((1 - c) * HALF + p * SH, SH), SH)
        tpeer[p] = bgs[:, other].T
        bgt[c, p, :, my_lane] = bgs[:, mine].T
        return 0

    lax.fori_loop(0, CH, flip, 0)
    k_peer = put(tpeer, bgt.at[1 - c, :, :, my_lane], to_c)
    load_y.start()
    load_x.start()
    got(k_peer, bgt.at[c, :, :, peer_lane])

    def bg_ref(h):
        def ref(z_, x_, first, last):
            lanes = pl.ds(pl.multiple_of((z_ * NX + x_) * 2 * SH, 2 * SH), 2 * SH)
            return bgt.at[c, first:last, pl.ds(h * HS, HS), lanes]

        return ref

    gb = [Gather(bg_ref(h), CH, BG_A, CH // 2, (CH + BG_A) // 2) for h in range(2)]
    gb[0].one()
    k_y = put(y_src, yb.at[my_tok], to_c)
    k_x = put(x_src, xb.at[my_tok], to_c)

    def grad(h, first, last):
        def rotate(t, _):
            rows = pl.ds(pl.multiple_of(t * WIDE, WIDE), WIDE)
            left = bgt[c, :, pl.ds(h * HS, HS), :].reshape(CH * HS, W)
            ygt[:, rows] = nt(left, yb[rows, :]).astype(BF)
            return 0

        lax.fori_loop(first, last, rotate, 0)

    def outer(h, first, last):
        def project(t, _):
            cols = pl.ds(pl.multiple_of(t * WIDE, WIDE), WIDE)
            vt[h, :, :, :, cols] = nn(ygt[...], xb[:, cols]).astype(BF).reshape(NZ, NX, HS, WIDE)
            return 0

        lax.fori_loop(first, last, project, 0)

    A, B = pl.ds(0, RS_A), pl.ds(RS_A, W - RS_A)
    B0, B1 = pl.ds(RS_A, (W - RS_A) // 2), pl.ds((W + RS_A) // 2, (W - RS_A) // 2)
    H0, H1 = pl.ds(0, W // 2), pl.ds(W // 2, W // 2)

    def plus(a, b):
        return (a.astype(F32) + b.astype(F32)).astype(BF)

    class Scatter:
        def __init__(self, h):
            self.h = h

        def one(self):
            h, o = self.h, 1 - zh
            self.z2 = put(vt.at[h, o, x2, :, A], rz.at[h, 0], to_z)
            self.bd0 = put(vt.at[h, o, x2, :, B0], rbd.at[h, 0], to_xp)
            self.bd1 = put(vt.at[h, o, x2, :, B1], rbd.at[h, 1], to_xm)
            self.od1 = put(vt.at[h, zh, x2, :, H1], rod.at[h, 1], to_xm)
            self.zp = put(vt.at[h, o, xp, :, A], rz.at[h, 1], to_z)
            self.zq = put(vt.at[h, o, xm, :, A], rz.at[h, 2], to_z)
            self.zo = put(vt.at[h, o, x, :, A], rz.at[h, 3], to_z)

        def two(self):
            h, o = self.h, 1 - zh
            got(self.z2, rz.at[h, 0])
            vt[h, zh, x2, :, A] = plus(vt[h, zh, x2, :, A], rz[h, 0])
            self.od0 = put(vt.at[h, zh, x2, :, H0], rod.at[h, 0], to_xp)
            got(self.bd0, rbd.at[h, 0])
            vt[h, o, xp, :, B0] = plus(vt[h, o, xp, :, B0], rbd[h, 0])
            self.bf0 = put(vt.at[h, o, xp, :, B], rbf.at[h, 0], to_xp)
            got(self.bd1, rbd.at[h, 1])
            vt[h, o, xm, :, B1] = plus(vt[h, o, xm, :, B1], rbd[h, 1])
            self.bf1 = put(vt.at[h, o, xm, :, B], rbf.at[h, 1], to_xm)

        def three(self):
            h, o = self.h, 1 - zh
            got(self.zq, rz.at[h, 2])
            vt[h, zh, xm, :, A] = plus(vt[h, zh, xm, :, A], rz[h, 2])
            got(self.od1, rod.at[h, 1])
            vt[h, zh, xm, :, H1] = plus(vt[h, zh, xm, :, H1], rod[h, 1])
            self.of1 = put(vt.at[h, zh, xm], rof.at[h, 1], to_xm)
            got(self.zp, rz.at[h, 1])
            vt[h, zh, xp, :, A] = plus(vt[h, zh, xp, :, A], rz[h, 1])
            got(self.od0, rod.at[h, 0])
            vt[h, zh, xp, :, H0] = plus(vt[h, zh, xp, :, H0], rod[h, 0])
            self.of0 = put(vt.at[h, zh, xp], rof.at[h, 0], to_xp)
            got(self.bf0, rbf.at[h, 0])
            got(self.bf1, rbf.at[h, 1])
            t = vt[h, o, x, :, B].astype(F32) + rbf[h, 0].astype(F32) + rbf[h, 1].astype(F32)
            vt[h, o, x, :, B] = t.astype(BF)
            self.zb = put(vt.at[h, o, x, :, B], rzb.at[h], to_z)

        def done(self):
            h = self.h
            got(self.zo, rz.at[h, 3])
            got(self.of0, rof.at[h, 0])
            got(self.of1, rof.at[h, 1])
            got(self.zb, rzb.at[h])
            t = vt[h, zh, x].astype(F32) + rof[h, 0].astype(F32) + rof[h, 1].astype(F32)
            rows = pl.ds(h * HS, HS)
            vtf[rows, A] = t[:, :RS_A] + rz[h, 3].astype(F32)
            vtf[rows, B] = t[:, RS_A:] + rzb[h].astype(F32)

    sc = [Scatter(h) for h in range(2)]

    def ba_part(y_):
        return ba.at[:, :, c, y_]

    def ba_theirs(y_):
        return ba.at[:, :, 1 - c, y_]

    ga.two()
    gb[0].two()
    ga.three()
    gb[1].one()
    ga.done()
    k_yp = put(ba_part(y), ba_part(y), to_yp)
    k_ym = put(ba_part(y), ba_part(y), to_ym)
    gb[0].three()
    gb[1].two()
    load_y.wait()
    load_x.wait()
    got(k_y, yb.at[other_tok])
    got(k_x, xb.at[other_tok])
    k_c = [put(ba_part(y), ba_part(y), to_c)]
    gb[0].done()
    grad(0, 0, 2)
    gb[1].three()
    grad(0, 2, 4)
    outer(0, 0, 4)
    sc[0].one()
    gb[1].done()
    k_bg = put(bgt.at[c], bgt.at[c], to_c)
    got(k_yp, ba_part(ym))
    k_yp2 = put(ba.at[0, :, c, ym], ba.at[0, :, c, ym], to_yp)
    got(k_ym, ba_part(yp))
    k_ym2 = put(ba.at[1, :, c, yp], ba.at[1, :, c, yp], to_ym)
    k_c += [put(ba_part(ym), ba_part(ym), to_c), put(ba_part(yp), ba_part(yp), to_c)]
    grad(1, 0, 4)
    sc[0].two()
    outer(1, 0, 2)
    sc[0].three()
    outer(1, 2, 4)
    sc[1].one()
    got(k_yp2, ba.at[0, :, c, y2])
    got(k_ym2, ba.at[1, :, c, y2])
    k_c.append(put(ba_part(y2), ba_part(y2), to_c))
    sc[1].two()
    sc[0].done()
    sc[1].three()
    for k, y_ in zip(k_c, (y, ym, yp, y2)):
        got(k, ba_theirs(y_))
    sc[1].done()

    own = vtf[...].astype(BF)
    my_m = pl.ds(pl.multiple_of(c * HALF + q * SH, SH), SH)
    lam_g = jnp.broadcast_to(row_of(eg_ref[:, my_m], y), (SH, SH)).T[:, 0:1]
    vtb = sct
    vtb[0] = own

    def scale(t, _):
        cols = pl.ds(pl.multiple_of(t * WIDE, WIDE), WIDE)
        inner = nn(vtb[0], ba[:, :, :, :, :, cols].reshape(W, WIDE))
        lam = row_of(ea_ref[:, cols], zl)
        vtb[1, :, cols] = (inner / (lam_g * lam + DAMPING)).astype(BF)
        return 0

    lax.fori_loop(0, W // WIDE, scale, 0)

    def back_rows(r):
        left = ba.reshape(W, W)[pl.ds(ROWS[r], SIZE[r]), :]
        back[c, zh, x, pl.ds(ROWS[r], SIZE[r]), :] = nt(left, vtb[1]).astype(BF)

    def back_ref(r):
        return lambda z_, x_, first, last: back.at[c, z_, x_, pl.ds(ROWS[r] + first, last - first)]

    gr = [Gather(back_ref(r), SIZE[r], LAST_Z[r], SIZE[r] // 2, (SIZE[r] + LAST_Z[r]) // 2) for r in range(R)]

    def to_core(r):
        rows = pl.ds(ROWS[r], SIZE[r])
        return put(back.at[c, :, :, rows], back.at[c, :, :, rows], to_c)

    def finish(r, part):
        rows = pl.ds(ROWS[r], SIZE[r])

        def block(t, _):
            cols = pl.ds(pl.multiple_of(t * WIDE, WIDE), WIDE)
            left = jnp.concatenate([back[k // CH, (k // NX) % NZ, k % NX, rows, :] for k in range(NC * CH)], axis=1)
            xb[rows, cols] = nn(left, bgt[:, :, :, cols].reshape(W, WIDE)).astype(BF)
            return 0

        half = W // 2
        lax.fori_loop(part * half // WIDE, (part + 1) * half // WIDE, block, 0)

    k3 = {}
    for r in range(R):
        back_rows(r)
        if r < 2:
            gr[r].one()
    got(k_bg, bgt.at[1 - c])
    for r in range(R + 3):
        if r < R:
            gr[r].two()
        if r + 2 < R:
            gr[r + 2].one()
        if r >= 3:
            got(k3[r - 3], back.at[1 - c, :, :, pl.ds(ROWS[r - 3], SIZE[r - 3])])
            finish(r - 3, 0)
        if 1 <= r <= R:
            gr[r - 1].three()
        if 2 <= r <= R + 1:
            gr[r - 2].done()
            k3[r - 2] = to_core(r - 2)
        if r >= 3:
            finish(r - 3, 1)
    for cp in sends:
        cp.wait_send()


def store(src, dst, sem):
    copies = []
    for k in range(PARTS):
        rows = pl.ds(k * (W // PARTS), W // PARTS)
        copies.append(pltpu.make_async_copy(src.at[rows], dst.at[rows], sem.at[k]))
        copies[-1].start()
    for cp in copies:
        cp.wait()


def body(inputs, out_grads, basis_g, basis_a, eig_g, eig_a):
    out = pl.pallas_call(
        kernel,
        out_shape=pltpu.VMEM((W, W), BF),
        in_specs=[pl.BlockSpec(memory_space=pl.ANY)] * 4 + [pl.BlockSpec(memory_space=pltpu.VMEM)] * 2,
        out_specs=pl.BlockSpec(memory_space=pltpu.VMEM),
        scratch_shapes=[
            pltpu.VMEM((NC * TOK, W), BF),
            pltpu.VMEM((SH, W), BF),
            pltpu.VMEM((CH, SH, SH), BF),
            pltpu.VMEM((NC, CH, SH, W), BF),
            pltpu.VMEM((NZ, NX, NC, NY, SH // NY, W), BF),
            pltpu.VMEM((CH * HS, NC * TOK), BF),
            pltpu.VMEM((2, NZ, NX, HS, W), BF),
            pltpu.VMEM((2, NX, HS, RS_A), BF),
            pltpu.VMEM((2, 2, HS, (W - RS_A) // 2), BF),
            pltpu.VMEM((2, 2, HS, W // 2), BF),
            pltpu.VMEM((2, 2, HS, W - RS_A), BF),
            pltpu.VMEM((2, 2, HS, W), BF),
            pltpu.VMEM((2, HS, W - RS_A), BF),
            pltpu.VMEM((SH, W), F32),
            pltpu.VMEM((2, SH, W), BF),
            pltpu.VMEM((NC, NZ, NX, W, SH), BF),
            pltpu.SemaphoreType.DMA((N_SEM,)),
            pltpu.SemaphoreType.DMA((N_SEM,)),
            pltpu.SemaphoreType.DMA((4,)),
        ],
        compiler_params=pltpu.CompilerParams(collective_id=0, has_side_effects=True, vmem_limit_bytes=51 * 2**20),
        cost_estimate=pl.CostEstimate(flops=2 * W * W * W * 3, bytes_accessed=40 * 2**20, transcendentals=0),
        name="precondition",
    )(inputs, out_grads, basis_g, basis_a, eig_g, eig_a)
    out = pl.pallas_call(
        store,
        out_shape=jax.ShapeDtypeStruct((W, W), BF),
        in_specs=[pl.BlockSpec(memory_space=pl.ANY)],
        out_specs=pl.BlockSpec(memory_space=pl.ANY),
        scratch_shapes=[pltpu.SemaphoreType.DMA((PARTS,))],
        compiler_params=pltpu.CompilerParams(vmem_limit_bytes=2**20),
        name="store",
    )(pltpu.with_memory_space_constraint(out, pltpu.VMEM))
    return out.reshape(W, 1, W)


def solution(mesh):
    in_specs = (P("dp", None), P("dp", None), P(None, "dp", None), P(None, "dp", None), P(), P())
    out_specs = P(None, "grad", None)
    return jax.shard_map(body, mesh=mesh, in_specs=in_specs, out_specs=out_specs, check_vma=False)
```

```python
import functools

import jax
import jax.numpy as jnp
from jax import lax
from jax.experimental import pallas as pl
from jax.experimental.pallas import tpu as pltpu
from jax.sharding import PartitionSpec as P

DAMPING = 0.05
MESH = pl.DeviceIdType.MESH
BF, F32 = jnp.bfloat16, jnp.float32

NX, NZ, NY, NC = 4, 2, 4, 2
CH = NX * NZ
W = 2048
SH = W // (CH * NC)
HALF = W // NC
HS = (80, 48)
HO = (0, 80)
TOK = 1024
BG_A = 4
RS_A = 768
WIDE = 512
SIZE = (512, 512, 512, 256, 256)
R = len(SIZE)
ROWS = tuple(sum(SIZE[:r]) for r in range(R))
LAST_Z = tuple(n * 7 // 16 // 32 * 32 for n in SIZE)
N_SEM = 160
PARTS = 8


def nn(a, b):
    return lax.dot_general(a, b, (((1,), (0,)), ((), ())), preferred_element_type=F32)


def nt(a, b):
    return lax.dot_general(a, b, (((1,), (1,)), ((), ())), preferred_element_type=F32)


def row_of(table, k):
    rows = lax.broadcasted_iota(jnp.int32, table.shape, 0)
    return jnp.sum(jnp.where(rows == k, table, 0.0), axis=0, keepdims=True)


def kernel(x_hbm, y_hbm, bg_hbm, ba_hbm, eg_ref, ea_ref, xb,
           yb, bgs, tpeer, bgt, ba, ygt, vt, rz, rbd, rod, rbf, rof, rzb, vtf, sct, back,
           ss, rs, ls):
    d = lax.axis_index("dp")
    g = lax.axis_index("grad")
    c = lax.rem(d, NC)
    x = lax.rem(lax.div(d, NC), NX)
    zh = lax.div(d, NC * NX)
    y = lax.rem(g, NY)
    zl = lax.div(g, NY)
    q = zh * NX + x

    def dp_of(z_, x_, c_):
        return (z_ * NX + x_) * NC + c_

    xp, xm, x2 = lax.rem(x + 1, NX), lax.rem(x + NX - 1, NX), lax.rem(x + 2, NX)
    to_xp, to_xm = (dp_of(zh, xp, c), g), (dp_of(zh, xm, c), g)
    to_z = (dp_of(1 - zh, x, c), g)
    to_c = (dp_of(zh, x, 1 - c), g)
    yp, ym, y2 = lax.rem(y + 1, NY), lax.rem(y + NY - 1, NY), lax.rem(y + 2, NY)
    to_yp, to_ym = (d, zl * NY + yp), (d, zl * NY + ym)

    sends = []
    count = [0]

    def slot():
        count[0] += 1
        return count[0] - 1

    def put(src, dst, dev):
        k = slot()
        cp = pltpu.make_async_remote_copy(src_ref=src, dst_ref=dst, send_sem=ss.at[k], recv_sem=rs.at[k],
                                          device_id=dev, device_id_type=MESH)
        cp.start()
        sends.append(cp)
        return k

    def got(k, dst):
        pltpu.make_async_remote_copy(src_ref=dst, dst_ref=dst, send_sem=ss.at[k], recv_sem=rs.at[k],
                                     device_id=to_c, device_id_type=MESH).wait_recv()

    load_bg = pltpu.make_async_copy(bg_hbm.at[y], bgs, ls.at[0])
    load_bg.start()
    x_src = x_hbm.at[:, pl.ds(pl.multiple_of(zl * W, W), W)]
    y_src = y_hbm.at[:, pl.ds(pl.multiple_of(y * W, W), W)]
    my_tok = pl.ds(pl.multiple_of(c * TOK, TOK), TOK)
    other_tok = pl.ds(pl.multiple_of((1 - c) * TOK, TOK), TOK)
    load_y = pltpu.make_async_copy(y_src, yb.at[my_tok], ls.at[1])
    load_x = pltpu.make_async_copy(x_src, xb.at[my_tok], ls.at[2])
    quarter = pl.ds(pl.multiple_of(y * (SH // NY), SH // NY), SH // NY)
    load_ba = pltpu.make_async_copy(ba_hbm.at[zl, quarter], ba.at[zh, x, c, y], ls.at[3])
    load_ba.start()

    barrier = pltpu.get_barrier_semaphore()
    partners = [to_xp, to_xm, to_z, to_c, to_yp, to_ym]
    for dev in partners:
        pl.semaphore_signal(barrier, inc=1, device_id=dev, device_id_type=MESH)
    pl.semaphore_wait(barrier, len(partners))

    class Gather:
        def __init__(self, ref, n, a, m, mb):
            self.ref, self.n, self.a, self.m, self.mb = ref, n, a, m, mb

        def move(self, z_, x_, first, last, dev):
            return put(self.ref(z_, x_, first, last), self.ref(z_, x_, first, last), dev)

        def one(self):
            self.p = self.move(zh, x, 0, self.n, to_xp)
            self.q = self.move(zh, x, 0, self.n, to_xm)
            self.z = self.move(zh, x, 0, self.n, to_z)

        def two(self):
            n, a, m = self.n, self.a, self.m
            got(self.p, self.ref(zh, xm, 0, n))
            self.p2 = self.move(zh, xm, 0, m, to_xp)
            self.zp = self.move(zh, xm, 0, a, to_z)
            got(self.q, self.ref(zh, xp, 0, n))
            self.q2 = self.move(zh, xp, m, n, to_xm)
            self.zq = self.move(zh, xp, 0, a, to_z)
            got(self.z, self.ref(1 - zh, x, 0, n))
            self.pb = self.move(1 - zh, x, a, n, to_xp)
            self.qb = self.move(1 - zh, x, a, n, to_xm)

        def three(self):
            n, a, m, mb = self.n, self.a, self.m, self.mb
            got(self.p2, self.ref(zh, x2, 0, m))
            self.z2 = self.move(zh, x2, 0, a, to_z)
            got(self.pb, self.ref(1 - zh, xm, a, n))
            self.pb2 = self.move(1 - zh, xm, a, mb, to_xp)
            got(self.qb, self.ref(1 - zh, xp, a, n))
            self.qb2 = self.move(1 - zh, xp, mb, n, to_xm)

        def done(self):
            n, a, m, mb = self.n, self.a, self.m, self.mb
            got(self.q2, self.ref(zh, x2, m, n))
            got(self.zp, self.ref(1 - zh, xm, 0, a))
            got(self.zq, self.ref(1 - zh, xp, 0, a))
            got(self.z2, self.ref(1 - zh, x2, 0, a))
            got(self.pb2, self.ref(1 - zh, x2, a, mb))
            got(self.qb2, self.ref(1 - zh, x2, mb, n))

    load_ba.wait()
    ga = Gather(lambda z_, x_, first, last: ba.at[z_, x_, c, y, :, first:last], W, W // 2, W // 2, 3 * W // 4)
    ga.one()

    load_bg.wait()
    my_lane = pl.ds(pl.multiple_of(q * 2 * SH + c * SH, SH), SH)
    peer_lane = pl.ds(pl.multiple_of(q * 2 * SH + (1 - c) * SH, SH), SH)

    def flip(p, _):
        mine = pl.ds(pl.multiple_of(c * HALF + p * SH, SH), SH)
        other = pl.ds(pl.multiple_of((1 - c) * HALF + p * SH, SH), SH)
        tpeer[p] = bgs[:, other].T
        bgt[c, p, :, my_lane] = bgs[:, mine].T
        return 0

    lax.fori_loop(0, CH, flip, 0)
    k_peer = put(tpeer, bgt.at[1 - c, :, :, my_lane], to_c)
    load_y.start()
    load_x.start()
    got(k_peer, bgt.at[c, :, :, peer_lane])

    def bg_ref(h):
        def ref(z_, x_, first, last):
            lanes = pl.ds(pl.multiple_of((z_ * NX + x_) * 2 * SH, 2 * SH), 2 * SH)
            return bgt.at[c, first:last, pl.ds(HO[h], HS[h]), lanes]

        return ref

    gb = [Gather(bg_ref(h), CH, BG_A, CH // 2, (CH + BG_A) // 2) for h in range(2)]
    gb[0].one()
    k_y = put(y_src, yb.at[my_tok], to_c)
    k_x = put(x_src, xb.at[my_tok], to_c)

    def grad(h, first, last):
        def rotate(t, _):
            rows = pl.ds(pl.multiple_of(t * WIDE, WIDE), WIDE)
            left = bgt[c, :, pl.ds(HO[h], HS[h]), :].reshape(CH * HS[h], W)
            ygt[pl.ds(0, CH * HS[h]), rows] = nt(left, yb[rows, :]).astype(BF)
            return 0

        lax.fori_loop(first, last, rotate, 0)

    def outer(h, first, last):
        def project(t, _):
            cols = pl.ds(pl.multiple_of(t * WIDE, WIDE), WIDE)
            prod = nn(ygt[pl.ds(0, CH * HS[h]), :], xb[:, cols]).astype(BF)
            vt[:, :, pl.ds(HO[h], HS[h]), cols] = prod.reshape(NZ, NX, HS[h], WIDE)
            return 0

        lax.fori_loop(first, last, project, 0)

    A, B = pl.ds(0, RS_A), pl.ds(RS_A, W - RS_A)
    B0, B1 = pl.ds(RS_A, (W - RS_A) // 2), pl.ds((W + RS_A) // 2, (W - RS_A) // 2)
    H0, H1 = pl.ds(0, W // 2), pl.ds(W // 2, W // 2)

    def plus(a, b):
        return (a.astype(F32) + b.astype(F32)).astype(BF)

    class Scatter:
        def __init__(self, h):
            self.r = pl.ds(HO[h], HS[h])

        def one_a(self):
            r, o = self.r, 1 - zh
            self.z2 = put(vt.at[o, x2, r, A], rz.at[0, r], to_z)
            self.zp = put(vt.at[o, xp, r, A], rz.at[1, r], to_z)
            self.zq = put(vt.at[o, xm, r, A], rz.at[2, r], to_z)
            self.zo = put(vt.at[o, x, r, A], rz.at[3, r], to_z)

        def one_b(self):
            r, o = self.r, 1 - zh
            self.bd0 = put(vt.at[o, x2, r, B0], rbd.at[0, r], to_xp)
            self.bd1 = put(vt.at[o, x2, r, B1], rbd.at[1, r], to_xm)
            self.od1 = put(vt.at[zh, x2, r, H1], rod.at[1, r], to_xm)

        def two(self):
            r, o = self.r, 1 - zh
            got(self.z2, rz.at[0, r])
            vt[zh, x2, r, A] = plus(vt[zh, x2, r, A], rz[0, r])
            self.od0 = put(vt.at[zh, x2, r, H0], rod.at[0, r], to_xp)
            got(self.bd0, rbd.at[0, r])
            vt[o, xp, r, B0] = plus(vt[o, xp, r, B0], rbd[0, r])
            self.bf0 = put(vt.at[o, xp, r, B], rbf.at[0, r], to_xp)
            got(self.bd1, rbd.at[1, r])
            vt[o, xm, r, B1] = plus(vt[o, xm, r, B1], rbd[1, r])
            self.bf1 = put(vt.at[o, xm, r, B], rbf.at[1, r], to_xm)

        def three(self):
            r, o = self.r, 1 - zh
            got(self.zq, rz.at[2, r])
            vt[zh, xm, r, A] = plus(vt[zh, xm, r, A], rz[2, r])
            got(self.od1, rod.at[1, r])
            vt[zh, xm, r, H1] = plus(vt[zh, xm, r, H1], rod[1, r])
            self.of1 = put(vt.at[zh, xm, r], rof.at[1, r], to_xm)
            got(self.zp, rz.at[1, r])
            vt[zh, xp, r, A] = plus(vt[zh, xp, r, A], rz[1, r])
            got(self.od0, rod.at[0, r])
            vt[zh, xp, r, H0] = plus(vt[zh, xp, r, H0], rod[0, r])
            self.of0 = put(vt.at[zh, xp, r], rof.at[0, r], to_xp)
            got(self.bf0, rbf.at[0, r])
            got(self.bf1, rbf.at[1, r])
            t = vt[o, x, r, B].astype(F32) + rbf[0, r].astype(F32) + rbf[1, r].astype(F32)
            vt[o, x, r, B] = t.astype(BF)
            self.zb = put(vt.at[o, x, r, B], rzb.at[r], to_z)

        def done(self):
            r = self.r
            got(self.zo, rz.at[3, r])
            got(self.of0, rof.at[0, r])
            got(self.of1, rof.at[1, r])
            got(self.zb, rzb.at[r])
            t = vt[zh, x, r].astype(F32) + rof[0, r].astype(F32) + rof[1, r].astype(F32)
            vtf[r, A] = t[:, :RS_A] + rz[3, r].astype(F32)
            vtf[r, B] = t[:, RS_A:] + rzb[r].astype(F32)

    sc = [Scatter(h) for h in range(2)]

    def ba_part(y_):
        return ba.at[:, :, c, y_]

    def ba_theirs(y_):
        return ba.at[:, :, 1 - c, y_]

    ga.two()
    gb[0].two()
    ga.three()
    gb[1].one()
    ga.done()
    k_yp = put(ba_part(y), ba_part(y), to_yp)
    k_ym = put(ba_part(y), ba_part(y), to_ym)
    gb[0].three()
    gb[1].two()
    load_y.wait()
    load_x.wait()
    got(k_y, yb.at[other_tok])
    got(k_x, xb.at[other_tok])
    k_c = [put(ba_part(y), ba_part(y), to_c)]
    gb[0].done()
    grad(0, 0, 2)
    gb[1].three()
    grad(0, 2, 4)
    outer(0, 0, 2)
    sc[0].one_a()
    got(k_yp, ba_part(ym))
    k_yp2 = put(ba.at[0, :, c, ym], ba.at[0, :, c, ym], to_yp)
    got(k_ym, ba_part(yp))
    k_ym2 = put(ba.at[1, :, c, yp], ba.at[1, :, c, yp], to_ym)
    k_c += [put(ba_part(ym), ba_part(ym), to_c), put(ba_part(yp), ba_part(yp), to_c)]
    outer(0, 2, 4)
    sc[0].one_b()
    gb[1].done()
    k_bg = put(bgt.at[c], bgt.at[c], to_c)
    grad(1, 0, 2)
    sc[0].two()
    grad(1, 2, 4)
    outer(1, 0, 1)
    sc[0].three()
    outer(1, 1, 2)
    sc[1].one_a()
    outer(1, 2, 4)
    sc[1].one_b()
    sc[0].done()
    sc[1].two()
    sc[1].three()
    got(k_yp2, ba.at[0, :, c, y2])
    got(k_ym2, ba.at[1, :, c, y2])
    k_c.append(put(ba_part(y2), ba_part(y2), to_c))
    for k, y_ in zip(k_c, (y, ym, yp, y2)):
        got(k, ba_theirs(y_))
    sc[1].done()

    own = vtf[...].astype(BF)
    my_m = pl.ds(pl.multiple_of(c * HALF + q * SH, SH), SH)
    lam_g = jnp.broadcast_to(row_of(eg_ref[:, my_m], y), (SH, SH)).T[:, 0:1]
    vtb = sct
    vtb[0] = own

    def scale(t, _):
        cols = pl.ds(pl.multiple_of(t * WIDE, WIDE), WIDE)
        inner = nn(vtb[0], ba[:, :, :, :, :, cols].reshape(W, WIDE))
        lam = row_of(ea_ref[:, cols], zl)
        vtb[1, :, cols] = (inner / (lam_g * lam + DAMPING)).astype(BF)
        return 0

    lax.fori_loop(0, W // WIDE, scale, 0)

    def back_rows(r):
        left = ba.reshape(W, W)[pl.ds(ROWS[r], SIZE[r]), :]
        back[c, zh, x, pl.ds(ROWS[r], SIZE[r]), :] = nt(left, vtb[1]).astype(BF)

    def back_ref(r):
        return lambda z_, x_, first, last: back.at[c, z_, x_, pl.ds(ROWS[r] + first, last - first)]

    gr = [Gather(back_ref(r), SIZE[r], LAST_Z[r], SIZE[r] // 2, (SIZE[r] + LAST_Z[r]) // 2) for r in range(R)]

    def to_core(r):
        rows = pl.ds(ROWS[r], SIZE[r])
        return put(back.at[c, :, :, rows], back.at[c, :, :, rows], to_c)

    def finish(r, part):
        rows = pl.ds(ROWS[r], SIZE[r])

        def block(t, _):
            cols = pl.ds(pl.multiple_of(t * WIDE, WIDE), WIDE)
            left = jnp.concatenate([back[k // CH, (k // NX) % NZ, k % NX, rows, :] for k in range(NC * CH)], axis=1)
            xb[rows, cols] = nn(left, bgt[:, :, :, cols].reshape(W, WIDE)).astype(BF)
            return 0

        half = W // 2
        lax.fori_loop(part * half // WIDE, (part + 1) * half // WIDE, block, 0)

    k3 = {}
    for r in range(R):
        back_rows(r)
        if r < 2:
            gr[r].one()
    got(k_bg, bgt.at[1 - c])
    for r in range(R + 3):
        if r < R:
            gr[r].two()
        if r + 2 < R:
            gr[r + 2].one()
        if r >= 3:
            got(k3[r - 3], back.at[1 - c, :, :, pl.ds(ROWS[r - 3], SIZE[r - 3])])
            finish(r - 3, 0)
        if 1 <= r <= R:
            gr[r - 1].three()
        if 2 <= r <= R + 1:
            gr[r - 2].done()
            k3[r - 2] = to_core(r - 2)
        if r >= 3:
            finish(r - 3, 1)
    for cp in sends:
        cp.wait_send()


def store(src, dst, sem):
    copies = []
    for k in range(PARTS):
        rows = pl.ds(k * (W // PARTS), W // PARTS)
        copies.append(pltpu.make_async_copy(src.at[rows], dst.at[rows], sem.at[k]))
        copies[-1].start()
    for cp in copies:
        cp.wait()


def body(inputs, out_grads, basis_g, basis_a, eig_g, eig_a):
    out = pl.pallas_call(
        kernel,
        out_shape=pltpu.VMEM((W, W), BF),
        in_specs=[pl.BlockSpec(memory_space=pl.ANY)] * 4 + [pl.BlockSpec(memory_space=pltpu.VMEM)] * 2,
        out_specs=pl.BlockSpec(memory_space=pltpu.VMEM),
        scratch_shapes=[
            pltpu.VMEM((NC * TOK, W), BF),
            pltpu.VMEM((SH, W), BF),
            pltpu.VMEM((CH, SH, SH), BF),
            pltpu.VMEM((NC, CH, SH, W), BF),
            pltpu.VMEM((NZ, NX, NC, NY, SH // NY, W), BF),
            pltpu.VMEM((CH * max(HS), NC * TOK), BF),
            pltpu.VMEM((NZ, NX, SH, W), BF),
            pltpu.VMEM((NX, SH, RS_A), BF),
            pltpu.VMEM((2, SH, (W - RS_A) // 2), BF),
            pltpu.VMEM((2, SH, W // 2), BF),
            pltpu.VMEM((2, SH, W - RS_A), BF),
            pltpu.VMEM((2, SH, W), BF),
            pltpu.VMEM((SH, W - RS_A), BF),
            pltpu.VMEM((SH, W), F32),
            pltpu.VMEM((2, SH, W), BF),
            pltpu.VMEM((NC, NZ, NX, W, SH), BF),
            pltpu.SemaphoreType.DMA((N_SEM,)),
            pltpu.SemaphoreType.DMA((N_SEM,)),
            pltpu.SemaphoreType.DMA((4,)),
        ],
        compiler_params=pltpu.CompilerParams(collective_id=0, has_side_effects=True, vmem_limit_bytes=51 * 2**20),
        cost_estimate=pl.CostEstimate(flops=2 * W * W * W * 3, bytes_accessed=40 * 2**20, transcendentals=0),
        name="precondition",
    )(inputs, out_grads, basis_g, basis_a, eig_g, eig_a)
    out = pl.pallas_call(
        store,
        out_shape=jax.ShapeDtypeStruct((W, W), BF),
        in_specs=[pl.BlockSpec(memory_space=pl.ANY)],
        out_specs=pl.BlockSpec(memory_space=pl.ANY),
        scratch_shapes=[pltpu.SemaphoreType.DMA((PARTS,))],
        compiler_params=pltpu.CompilerParams(vmem_limit_bytes=2**20),
        name="store",
    )(pltpu.with_memory_space_constraint(out, pltpu.VMEM))
    return out.reshape(W, 1, W)


def solution(mesh):
    in_specs = (P("dp", None), P("dp", None), P(None, "dp", None), P(None, "dp", None), P(), P())
    out_specs = P(None, "grad", None)
    return jax.shard_map(body, mesh=mesh, in_specs=in_specs, out_specs=out_specs, check_vma=False)
```
